32 devices in a mesh: groups: 2 (over y), blk: 16 (over z, x, core).
Axes of the slice: x: 2, y: 2, z: 4, core: 2. Of those that a mesh axis runs over, the one named last changes fastest.
Arguments:
- train_rows: bfloat16 [8192, 8192], P(('groups', 'blk')), parts along dimension 0, may hold values from -6 to 6
- pair_ids: int32 [8192], P(('groups', 'blk')), parts along dimension 0, may hold values from 0 to 127, as said below
- pair_owner: int32 [4096, 1], P(('groups', 'blk')), parts along dimension 0, may hold values from 0 to 15; in each aligned block of 128 rows (0 to 127, 128 to 255, ...) at most 16 rows name the same one
- second_moment: float32 [8192], replicated, may hold values from 0.0001 to 0.1
- val_rows: bfloat16 [128, 8192], P('blk'), may hold values from -6 to 6
Outputs:
- influence: bfloat16 [16384, 128], P(('groups', 'blk')), parts along dimension 0
- order_gap: bfloat16 [8192, 128], P(('groups', 'blk')), parts along dimension 0
The draws below stay inside these ranges and needn't reach their ends.
There are 2 independent parts, one for each index of `groups`. The reference program is written for one: setup_inputs(seed, part) draws one part's arguments, and reference() takes and returns one part's arrays. A program takes and returns all parts, laid end to end along the dimension named above; an argument that names none is the same for every part. Nothing has to cross between parts.
Inputs may be any that keep to these rules, and one draw needn't show every extreme that they name: `pair_ids`: within each aligned block of 256 rows every pair number appears exactly twice; the first appearance is the forward order, the second the swapped one. `pair_owner`: within the 128 pairs of one device no owner is named more than 16 times.
All inputs are finite; a program needn't handle non-finite values.
Results may differ from the reference program's by a relative error of at most 0.0065.
Values may be sent and summed in bfloat16 or wider, within the bound.
A program may use at most 128 MiB of HBM per device.

```python
import math
import jax
import jax.numpy as jnp
import numpy as np
from jax import lax

K = 8192
SRC_DEV = 256
PAIRS_DEV = 128
PEER_CAP = 16
SLOTS_DEV = 512
TRAIN = 4096
PAIRS = 2048
VAL = 128
N_BLK = 16


def draw_pair_ids(key, part):
    key = jax.random.fold_in(key, 11)
    streams = jax.random.split(key, N_BLK)
    orders = jax.vmap(lambda stream: jax.random.permutation(stream, SRC_DEV))(streams)
    return (orders // 2).reshape(-1).astype(jnp.int32)


def levels(key, shape, shards, least, top_value):
    level = 1.0
    for axis_at, blocks in shards:
        steps = jax.random.uniform(jax.random.fold_in(jax.random.fold_in(key, 6), axis_at), (blocks,), jnp.float32, least / len(shards), top_value / len(shards))
        level = level * jnp.repeat(jnp.exp(steps), shape[axis_at] // blocks).reshape((-1,) + (1,) * (len(shape) - 1 - axis_at))
    return level


def deal_out(key, own, number, rows, amount, top, bound, lean):
    ranking = jax.random.permutation(key, amount)
    crowded, ordinary = load_shares(amount, rows * top, bound, lean, True), load_shares(amount, rows * top, bound, lean, False)
    places = jnp.arange(amount)

    def named(tallies, rotation):
        used = int((tallies > 0).sum())
        fixed = max(1, used // 4)
        moved = fixed + (places - fixed + rotation * (used - fixed)) % max(1, amount - fixed)
        return jnp.zeros((amount,), jnp.int32).at[ranking[jnp.where(places < fixed, places, moved)]].set(jnp.asarray(tallies, jnp.int32))

    tallies = jnp.where(number % 4 == 0, named(crowded, number // 4), named(ordinary, number - number // 4 - 1))
    mixed = jax.random.permutation(jax.random.fold_in(own, 3), amount)
    giver, receiver = mixed[0:amount // 2 * 2:2], mixed[1:amount // 2 * 2:2]
    slack = jnp.minimum(tallies[giver] - 1, bound - tallies[receiver]) // 2
    slack = jnp.where((giver == ranking[0]) | (receiver == ranking[0]) | (tallies[receiver] == 0), 0, jnp.maximum(slack, 0))
    moved = jax.random.randint(jax.random.fold_in(own, 4), (amount // 2,), 0, 1 << 20) % (slack + 1)
    tallies = tallies.at[giver].add(-moved).at[receiver].add(moved)
    items = jnp.searchsorted(jnp.cumsum(tallies), jnp.arange(rows * top), side="right").astype(jnp.int32)
    table = items.reshape(top, rows).T
    table = table[jax.random.permutation(jax.random.fold_in(own, 1), rows)]
    rotation = jax.random.randint(jax.random.fold_in(own, 2), (rows, 1), 0, top)
    return jnp.take_along_axis(table, (jnp.arange(top)[None, :] + rotation) % top, axis=1)


def load_shares(number_of, total, bound, lean, full):
    portions = [(1 << 20) // math.isqrt(rank ** lean) + 1 for rank in range(1, number_of + 1)]
    largest = bound if full else min(bound, max(-(-total // number_of), total * portions[0] // sum(portions)))
    least = 1 if total - largest >= number_of - 1 else 0
    counts, rest = [largest] + [least] * (number_of - 1), total - largest - least * (number_of - 1)
    while rest > 0:
        movable = [i for i in range(1, number_of) if counts[i] < largest] or [i for i in range(1, number_of) if counts[i] < bound]
        whole, left = sum([portions[i] for i in movable]), rest
        for i in movable:
            extra = min(bound - counts[i], max(1, left * portions[i] // whole), rest)
            counts[i] = counts[i] + extra
            rest = rest - extra
    return np.array(counts)


def normal_values(key, dims, spread, most, pieces=(), kind=jnp.bfloat16):
    array = spread * jax.random.normal(key, dims, jnp.float32)
    if pieces:
        array = array * levels(key, dims, pieces, -0.22, 0.18)
    return jnp.clip(array, -most, most).astype(kind)


def setup_inputs(seed: int = 0, part: int = 0) -> dict:
    streams_of = jax.random.split(jax.random.key(seed), 6)
    part_splits = jax.random.split(jax.random.fold_in(streams_of[5], part), 6)
    train_rows = normal_values(part_splits[0], (TRAIN, K), 1.0, 6.0, ((0, 16),))
    pair_ids = draw_pair_ids(jax.random.fold_in(jax.random.fold_in(streams_of[5], part), 71), part)
    pair_owner_keys = jax.random.split(jax.random.fold_in(part_splits[2], 1), PAIRS // PAIRS_DEV)
    pair_owner_turns = jax.random.permutation(jax.random.fold_in(part_splits[2], 3), PAIRS // PAIRS_DEV)
    pair_owner = jax.vmap(lambda own, number: deal_out(jax.random.fold_in(part_splits[2], 2), own, number, PAIRS_DEV, N_BLK, 1, PEER_CAP, 2))(pair_owner_keys, pair_owner_turns).reshape((PAIRS, 1))
    second_moment = jnp.clip(jnp.exp(jax.random.uniform(streams_of[3], (K,), jnp.float32, math.log(0.0001), math.log(0.1))), 0.0001, 0.1)
    val_rows = normal_values(streams_of[4], (VAL, K), 1.0, 6.0, ((0, 16),))
    return {"train_rows": train_rows, "pair_ids": pair_ids, "pair_owner": pair_owner, "second_moment": second_moment, "val_rows": val_rows}


epsilon = 1e-05

def unit_rows(rows):
    wide = rows.astype(jnp.float32)
    return (wide * lax.rsqrt(lax.optimization_barrier(jnp.mean(wide * wide, axis=1, keepdims=True)) + epsilon)).astype(jnp.bfloat16)

def reference(train_rows, pair_ids, pair_owner, second_moment, val_rows):
    members = N_BLK
    capacity = PEER_CAP
    owners = pair_owner[:, 0].reshape(members, PAIRS_DEV)
    owner_hot = (owners[:, :, None] == jnp.arange(members, dtype=jnp.int32)[None, None, :]).astype(jnp.int32)
    position = lax.optimization_barrier(jnp.sum((jnp.cumsum(owner_hot, axis=1) - owner_hot) * owner_hot, axis=2))
    pair_local = pair_ids.reshape(members, SRC_DEV)
    pair_hot = (pair_local[:, :, None] == jnp.arange(PAIRS_DEV, dtype=jnp.int32)[None, None, :]).astype(jnp.int32)
    second = lax.optimization_barrier(jnp.sum((jnp.cumsum(pair_hot, axis=1) - pair_hot) * pair_hot, axis=2))
    row_owner = jnp.take_along_axis(owners, pair_local, axis=1)
    row_position = jnp.take_along_axis(position, pair_local, axis=1)
    source = jnp.arange(members, dtype=jnp.int32)[:, None]
    slot_index = (row_owner * SLOTS_DEV + source * (2 * capacity) + 2 * row_position + second).astype(jnp.int32)
    precondition = 1.0 / (jnp.sqrt(second_moment) + 1e-08)
    scaled = (train_rows.astype(jnp.float32) * precondition[None, :]).astype(jnp.bfloat16)
    train_unit = unit_rows(scaled)
    val_unit = unit_rows(val_rows)
    live = lax.dot_general(train_unit, val_unit, (((1,), (1,)), ((), ())), preferred_element_type=jnp.float32) / math.sqrt(K)
    scores = jnp.zeros((members * SLOTS_DEV, VAL), jnp.float32).at[slot_index.reshape(-1)].set(live)
    paired = scores.reshape(-1, 2, VAL)
    return (scores.astype(jnp.bfloat16), (paired[:, 0] - paired[:, 1]).astype(jnp.bfloat16))
```

```python
import math

import jax
import jax.numpy as jnp
from jax import lax
from jax.sharding import PartitionSpec as P

epsilon = 1e-05


def unit_rows(rows):
    wide = rows.astype(jnp.float32)
    return (wide * lax.rsqrt(jnp.mean(wide * wide, axis=1, keepdims=True) + epsilon)).astype(
        jnp.bfloat16
    )


def on_device(train_rows, pair_ids, pair_owner, second_moment, val_rows):
    members = lax.axis_size("blk")
    row_total, features = train_rows.shape
    pair_total = row_total // 2
    capacity = max(2, 2 * pair_total // members)
    gathered = lax.all_gather(unit_rows(val_rows), "blk", axis=0, tiled=True)
    vals = gathered.shape[0]
    owner_hot = (pair_owner == jnp.arange(members, dtype=jnp.int32)[None, :]).astype(jnp.float32)
    before = jnp.tri(pair_total, k=-1, dtype=jnp.float32)
    position = jnp.sum(jnp.dot(before, owner_hot) * owner_hot, axis=1, keepdims=True)
    place = pair_owner.astype(jnp.float32) * (2 * capacity) + 2 * position
    pair_hot = (jnp.arange(pair_total, dtype=jnp.int32)[:, None] == pair_ids[None, :]).astype(jnp.float32)
    earlier = jnp.dot(pair_hot, jnp.tri(row_total, k=-1, dtype=jnp.float32).T)
    target = jnp.sum(pair_hot * (place + earlier), axis=0).astype(jnp.int32)
    slot_count = members * 2 * capacity
    hot = (jnp.arange(slot_count, dtype=jnp.int32)[:, None] == target[None, :]).astype(jnp.bfloat16)
    precondition = 1.0 / (jnp.sqrt(second_moment) + 1e-08)
    scaled = (train_rows.astype(jnp.float32) * precondition[None, :]).astype(jnp.bfloat16)
    live = lax.dot_general(
        unit_rows(scaled), gathered, (((1,), (1,)), ((), ())), preferred_element_type=jnp.float32
    ) / math.sqrt(features)
    high = live.astype(jnp.bfloat16)
    low = (live - high.astype(jnp.float32)).astype(jnp.bfloat16)
    influence = jnp.dot(hot, high, preferred_element_type=jnp.float32)
    rest = jnp.dot(hot, low, preferred_element_type=jnp.float32)
    paired = (influence + rest).reshape(-1, 2, vals)
    gap = paired[:, 0] - paired[:, 1]
    sent = jnp.concatenate(
        [
            influence.astype(jnp.bfloat16).reshape(members, 2 * capacity, vals),
            gap.astype(jnp.bfloat16).reshape(members, capacity, vals),
        ],
        axis=1,
    )
    arrived = lax.all_to_all(sent, "blk", split_axis=0, concat_axis=0, tiled=True)
    return (
        arrived[:, : 2 * capacity].reshape(slot_count, vals),
        arrived[:, 2 * capacity :].reshape(slot_count // 2, vals),
    )


def solution(mesh):
    return jax.shard_map(
        on_device,
        mesh=mesh,
        in_specs=(
            P(("groups", "blk"), None),
            P(("groups", "blk")),
            P(("groups", "blk"), None),
            P(),
            P("blk", None),
        ),
        out_specs=(P(("groups", "blk"), None), P(("groups", "blk"), None)),
        check_vma=False,
    )
```

```python
import functools
import math

import jax
import jax.numpy as jnp
from jax import lax
from jax.experimental import pallas as pl
from jax.experimental.pallas import tpu as pltpu
from jax.sharding import PartitionSpec as P

epsilon = 1e-05


def unit_rows(rows):
    wide = rows.astype(jnp.float32)
    return (wide * lax.rsqrt(jnp.mean(wide * wide, axis=1, keepdims=True) + epsilon)).astype(
        jnp.bfloat16
    )


def plain(train_rows, pair_ids, pair_owner, second_moment, val_rows):
    members = lax.axis_size("blk")
    row_total, features = train_rows.shape
    pair_total = row_total // 2
    capacity = max(2, 2 * pair_total // members)
    gathered = lax.all_gather(unit_rows(val_rows), "blk", axis=0, tiled=True)
    vals = gathered.shape[0]
    owner_hot = (pair_owner == jnp.arange(members, dtype=jnp.int32)[None, :]).astype(jnp.float32)
    before = jnp.tri(pair_total, k=-1, dtype=jnp.float32)
    position = jnp.sum(jnp.dot(before, owner_hot) * owner_hot, axis=1, keepdims=True)
    place = pair_owner.astype(jnp.float32) * (2 * capacity) + 2 * position
    pair_hot = (jnp.arange(pair_total, dtype=jnp.int32)[:, None] == pair_ids[None, :]).astype(jnp.float32)
    earlier = jnp.dot(pair_hot, jnp.tri(row_total, k=-1, dtype=jnp.float32).T)
    target = jnp.sum(pair_hot * (place + earlier), axis=0).astype(jnp.int32)
    slot_count = members * 2 * capacity
    hot = (jnp.arange(slot_count, dtype=jnp.int32)[:, None] == target[None, :]).astype(jnp.bfloat16)
    precondition = 1.0 / (jnp.sqrt(second_moment) + 1e-08)
    scaled = (train_rows.astype(jnp.float32) * precondition[None, :]).astype(jnp.bfloat16)
    live = lax.dot_general(
        unit_rows(scaled), gathered, (((1,), (1,)), ((), ())), preferred_element_type=jnp.float32
    ) / math.sqrt(features)
    high = live.astype(jnp.bfloat16)
    low = (live - high.astype(jnp.float32)).astype(jnp.bfloat16)
    influence = jnp.dot(hot, high, preferred_element_type=jnp.float32)
    rest = jnp.dot(hot, low, preferred_element_type=jnp.float32)
    paired = (influence + rest).reshape(-1, 2, vals)
    gap = paired[:, 0] - paired[:, 1]
    sent = jnp.concatenate(
        [
            influence.astype(jnp.bfloat16).reshape(members, 2 * capacity, vals),
            gap.astype(jnp.bfloat16).reshape(members, capacity, vals),
        ],
        axis=1,
    )
    arrived = lax.all_to_all(sent, "blk", split_axis=0, concat_axis=0, tiled=True)
    return (
        arrived[:, : 2 * capacity].reshape(slot_count, vals),
        arrived[:, 2 * capacity :].reshape(slot_count // 2, vals),
    )


MESH = pl.DeviceIdType.MESH
CHUNKS = 4
COLS = 2
STRIP = 16


def hot_places(ids, owners, capacity):
    pairs, rows = owners.shape[0], ids.shape[1]
    iota = lax.broadcasted_iota
    owner_hot = (iota(jnp.int32, (pairs, 128), 1) == owners).astype(jnp.float32)
    before = (iota(jnp.int32, (pairs, pairs), 1) < iota(jnp.int32, (pairs, pairs), 0)).astype(jnp.float32)
    counts = jnp.dot(before.astype(jnp.bfloat16), owner_hot.astype(jnp.bfloat16), preferred_element_type=jnp.float32)
    position = jnp.sum(counts * owner_hot, axis=1, keepdims=True)
    place = owners.astype(jnp.float32) * capacity + position
    pair_hot = (iota(jnp.int32, (pairs, rows), 0) == ids).astype(jnp.float32)
    after = (iota(jnp.int32, (rows, rows), 0) < iota(jnp.int32, (rows, rows), 1)).astype(jnp.float32)
    earlier = jnp.dot(pair_hot.astype(jnp.bfloat16), after.astype(jnp.bfloat16), preferred_element_type=jnp.float32)
    slot = jnp.sum(pair_hot * place, axis=0, keepdims=True)
    second = jnp.sum(pair_hot * earlier, axis=0, keepdims=True)
    return slot, second


def kernel(
    members, capacity,
    train_ref, ids_ref, owner_ref, moment_ref, val_ref,
    influence_ref, gap_ref,
    rows, pre, squares, held, hot, signed, outbox, inbox,
    row_sem, z_send, x_send, y_send, c_send, held_sem, out_send, out_recv,
):
    depth = members // (2 * COLS)
    total, features = train_ref.shape
    vals = val_ref.shape[0]
    wide = features // CHUNKS
    half = wide // 2
    slots = members * capacity
    me = lax.axis_index("blk")
    group = lax.axis_index("groups")
    core = lax.rem(me, 2)
    col = lax.rem(me // 2, COLS)
    layer = me // (2 * COLS)

    def at(dz, dx, dc=0):
        z = lax.rem(layer + dz, depth)
        x = lax.rem(col + dx, COLS)
        return (z * COLS + x) * 2 + lax.rem(core + dc, 2)

    here = (group, me)
    aside = (group, at(0, 1))
    across = (1 - group, me)
    sibling = (group, at(0, 0, 1))

    fetches = []
    for k in range(CHUNKS):
        lanes = pl.ds(k * wide, wide)
        copy = pltpu.make_async_copy(train_ref.at[:, lanes], rows.at[:, lanes], row_sem.at[k])
        copy.start()
        fetches.append(copy)

    barrier = pltpu.get_barrier_semaphore()
    for step in range(1, members):
        pl.semaphore_signal(barrier, 1, device_id=(group, lax.rem(me + step, members)), device_id_type=MESH)
    pl.semaphore_signal(barrier, 1, device_id=across, device_id_type=MESH)

    val = val_ref[...].astype(jnp.float32)
    unit = val * lax.rsqrt(jnp.mean(val * val, axis=1, keepdims=True) + epsilon)
    for k in range(CHUNKS):
        both = [unit[:, k * wide + h * half : k * wide + (h + 1) * half] for h in range(2)]
        held[k, pl.ds(me, 1)] = jnp.concatenate(both, axis=0).astype(jnp.bfloat16)[None]
    pl.semaphore_wait(barrier, members)

    sends = []

    def send(k, m, sem, to):
        copy = pltpu.make_async_remote_copy(
            src_ref=held.at[k, m], dst_ref=held.at[k, m], send_sem=sem, recv_sem=held_sem.at[k, m],
            device_id=to, device_id_type=MESH,
        )
        copy.start()
        sends.append(copy)

    def arrived(k, m):
        pltpu.make_async_remote_copy(
            src_ref=held.at[k, m], dst_ref=held.at[k, m], send_sem=out_send.at[0], recv_sem=held_sem.at[k, m],
            device_id=sibling, device_id_type=MESH,
        ).wait_recv()

    def to_core(k, dz, dx):
        send(k, at(dz, dx), c_send.at[k, dx * depth + dz], sibling)

    def to_side(k, dz):
        send(k, at(dz, 0), x_send.at[k, dz], aside)

    def to_group(k, dz, dx):
        send(k, at(dz, dx), y_send.at[k, dx * depth + dz], across)

    steps = range(1, depth)
    own = [2 * j + group for j in range(CHUNKS // 2)]
    other = [2 * j + 1 - group for j in range(CHUNKS // 2)]

    for j in range(CHUNKS // 2):
        for dz in steps:
            send(own[j], me, z_send.at[j, dz - 1], (group, at(dz, 0)))
        to_side(own[j], 0)
        if j % 2:
            to_side(other[j], 0)
        to_core(own[j], 0, 0)
        to_core(other[j], 0, 0)

    def from_z(j):
        for dz in steps:
            arrived(own[j], at(dz, 0))
            to_side(own[j], dz)
            to_group(own[j], dz, 0)
            to_core(own[j], dz, 0)

    def side_own(j):
        for dz in range(depth):
            arrived(own[j], at(dz, 1))
            if j % 2 == 0:
                to_group(own[j], dz, 1)
            to_core(own[j], dz, 1)

    def group_near(j):
        for dz in steps:
            arrived(other[j], at(dz, 0))
            if j % 2:
                to_side(other[j], dz)
            to_core(other[j], dz, 0)

    def far(j):
        for dz in range(depth):
            arrived(other[j], at(dz, 1))
            to_core(other[j], dz, 1)

    def from_core(j):
        for k in (own[j], other[j]):
            for dz in range(depth):
                for dx in range(COLS):
                    arrived(k, at(dz, dx, 1))

    def scale(k):
        fetches[k].wait()
        lanes = pl.ds(k * wide, wide)

        def strip(i, _):
            band = pl.ds(pl.multiple_of(i * STRIP, STRIP), STRIP)
            scaled = (rows[band, lanes].astype(jnp.float32) * pre[:, lanes]).astype(jnp.bfloat16)
            rows[band, lanes] = scaled
            scaled = scaled.astype(jnp.float32)
            found = jnp.sum(scaled * scaled, axis=1, keepdims=True)
            squares[band, :] = found if k == 0 else squares[band, :] + found
            return 0

        lax.fori_loop(0, total // STRIP, strip, 0)

    def product(k):
        block = held[k].astype(jnp.float32)
        result = None
        for h in range(2):
            piece = block[:, h * vals : (h + 1) * vals].reshape(members * vals, half).astype(jnp.bfloat16)
            left = rows[:, pl.ds(k * wide + h * half, half)]
            term = lax.dot_general(left, piece, (((1,), (1,)), ((), ())), preferred_element_type=jnp.float32)
            result = term if result is None else result + term
        return result

    pre[...] = 1.0 / (jnp.sqrt(moment_ref[...]) + 1e-08)
    scale(0)
    from_z(0)
    scale(1)
    side_own(0)
    from_z(1)
    scale(2)
    group_near(1)
    group_near(0)
    scale(3)
    side_own(1)
    far(0)
    slot, second = hot_places(ids_ref[...], owner_ref[...], capacity)
    place = lax.broadcasted_iota(jnp.int32, (2 * slots, total), 0).astype(jnp.float32)
    hot[...] = (place == 2 * slot + second).astype(jnp.float32).astype(jnp.bfloat16)
    place = lax.broadcasted_iota(jnp.int32, (slots, total), 0).astype(jnp.float32)
    signed[...] = jnp.where(place == slot, 1 - 2 * second, 0.0).astype(jnp.bfloat16)
    from_core(0)
    live = product(0) + product(1)
    far(1)
    from_core(1)
    live = live + product(2) + product(3)
    live = live * (lax.rsqrt(squares[...] / features + epsilon) / math.sqrt(features))

    high = live.astype(jnp.bfloat16)
    low = (live - high.astype(jnp.float32)).astype(jnp.bfloat16)
    influence = jnp.dot(hot[...], high, preferred_element_type=jnp.float32)
    gap = jnp.dot(signed[...], high, preferred_element_type=jnp.float32)
    gap = gap + jnp.dot(signed[...], low, preferred_element_type=jnp.float32)
    outbox[:, : 2 * capacity] = influence.astype(jnp.bfloat16).reshape(members, 2 * capacity, -1)
    outbox[:, 2 * capacity :] = gap.astype(jnp.bfloat16).reshape(members, capacity, -1)

    for step in range(1, members):
        to = lax.rem(me + step, members)
        copy = pltpu.make_async_remote_copy(
            src_ref=outbox.at[to], dst_ref=inbox.at[me], send_sem=out_send.at[step], recv_sem=out_recv.at[me],
            device_id=(group, to), device_id_type=MESH,
        )
        copy.start()
        sends.append(copy)

    def place_block(m, ref):
        influence_ref[pl.ds(pl.multiple_of(m * 2 * capacity, 2 * capacity), 2 * capacity), :] = ref[m, : 2 * capacity]
        gap_ref[pl.ds(pl.multiple_of(m * capacity, capacity), capacity), :] = ref[m, 2 * capacity :]

    place_block(me, outbox)
    for step in range(1, members):
        m = lax.rem(me + members - step, members)
        pltpu.make_async_remote_copy(
            src_ref=outbox.at[m], dst_ref=inbox.at[m], send_sem=out_send.at[0], recv_sem=out_recv.at[m],
            device_id=sibling, device_id_type=MESH,
        ).wait_recv()
        place_block(m, inbox)
    for copy in sends:
        copy.wait_send()


def on_device(train_rows, pair_ids, pair_owner, second_moment, val_rows):
    members = lax.axis_size("blk")
    total, features = train_rows.shape
    capacity = max(2, total // members)
    vals = val_rows.shape[0]
    if capacity % 16 or members % (2 * COLS) or lax.axis_size("groups") != 2:
        return plain(train_rows, pair_ids, pair_owner, second_moment, val_rows)
    slots, width, wide = members * capacity, members * vals, features // CHUNKS
    depth = members // (2 * COLS)
    vmem = pl.BlockSpec(memory_space=pltpu.VMEM)
    dma = pltpu.SemaphoreType.DMA
    return pl.pallas_call(
        functools.partial(kernel, members, capacity),
        out_shape=(
            jax.ShapeDtypeStruct((2 * slots, width), jnp.bfloat16),
            jax.ShapeDtypeStruct((slots, width), jnp.bfloat16),
        ),
        in_specs=[pl.BlockSpec(memory_space=pl.ANY), vmem, vmem, vmem, vmem],
        out_specs=(vmem, vmem),
        scratch_shapes=[
            pltpu.VMEM((total, features), jnp.bfloat16),
            pltpu.VMEM((1, features), jnp.float32),
            pltpu.VMEM((total, 1), jnp.float32),
            pltpu.VMEM((CHUNKS, members, 2 * vals, wide // 2), jnp.bfloat16),
            pltpu.VMEM((2 * slots, total), jnp.bfloat16),
            pltpu.VMEM((slots, total), jnp.bfloat16),
            pltpu.VMEM((members, 3 * capacity, width), jnp.bfloat16),
            pltpu.VMEM((members, 3 * capacity, width), jnp.bfloat16),
            dma((CHUNKS,)),
            dma((CHUNKS // 2, depth)),
            dma((CHUNKS, depth)),
            dma((CHUNKS, COLS * depth)),
            dma((CHUNKS, COLS * depth)),
            dma((CHUNKS, members)),
            dma((members,)),
            dma((members,)),
        ],
        compiler_params=pltpu.CompilerParams(
            collective_id=0, has_side_effects=True, vmem_limit_bytes=48 * 2**20
        ),
        cost_estimate=pl.CostEstimate(
            flops=2 * total * features * width, bytes_accessed=2 * total * features, transcendentals=0
        ),
    )(train_rows, pair_ids.reshape(1, total), pair_owner, second_moment.reshape(1, features), val_rows)


def solution(mesh):
    return jax.shard_map(
        on_device,
        mesh=mesh,
        in_specs=(
            P(("groups", "blk"), None),
            P(("groups", "blk")),
            P(("groups", "blk"), None),
            P(),
            P("blk", None),
        ),
        out_specs=(P(("groups", "blk"), None), P(("groups", "blk"), None)),
        check_vma=False,
    )
```

```python
import functools
import math

import jax
import jax.numpy as jnp
from jax import lax
from jax.experimental import pallas as pl
from jax.experimental.pallas import tpu as pltpu
from jax.sharding import PartitionSpec as P

epsilon = 1e-05


def unit_rows(rows):
    wide = rows.astype(jnp.float32)
    return (wide * lax.rsqrt(jnp.mean(wide * wide, axis=1, keepdims=True) + epsilon)).astype(
        jnp.bfloat16
    )


def plain(train_rows, pair_ids, pair_owner, second_moment, val_rows):
    members = lax.axis_size("blk")
    row_total, features = train_rows.shape
    pair_total = row_total // 2
    capacity = max(2, 2 * pair_total // members)
    gathered = lax.all_gather(unit_rows(val_rows), "blk", axis=0, tiled=True)
    vals = gathered.shape[0]
    owner_hot = (pair_owner == jnp.arange(members, dtype=jnp.int32)[None, :]).astype(jnp.float32)
    before = jnp.tri(pair_total, k=-1, dtype=jnp.float32)
    position = jnp.sum(jnp.dot(before, owner_hot) * owner_hot, axis=1, keepdims=True)
    place = pair_owner.astype(jnp.float32) * (2 * capacity) + 2 * position
    pair_hot = (jnp.arange(pair_total, dtype=jnp.int32)[:, None] == pair_ids[None, :]).astype(jnp.float32)
    earlier = jnp.dot(pair_hot, jnp.tri(row_total, k=-1, dtype=jnp.float32).T)
    target = jnp.sum(pair_hot * (place + earlier), axis=0).astype(jnp.int32)
    slot_count = members * 2 * capacity
    hot = (jnp.arange(slot_count, dtype=jnp.int32)[:, None] == target[None, :]).astype(jnp.bfloat16)
    precondition = 1.0 / (jnp.sqrt(second_moment) + 1e-08)
    scaled = (train_rows.astype(jnp.float32) * precondition[None, :]).astype(jnp.bfloat16)
    live = lax.dot_general(
        unit_rows(scaled), gathered, (((1,), (1,)), ((), ())), preferred_element_type=jnp.float32
    ) / math.sqrt(features)
    high = live.astype(jnp.bfloat16)
    low = (live - high.astype(jnp.float32)).astype(jnp.bfloat16)
    influence = jnp.dot(hot, high, preferred_element_type=jnp.float32)
    rest = jnp.dot(hot, low, preferred_element_type=jnp.float32)
    paired = (influence + rest).reshape(-1, 2, vals)
    gap = paired[:, 0] - paired[:, 1]
    sent = jnp.concatenate(
        [
            influence.astype(jnp.bfloat16).reshape(members, 2 * capacity, vals),
            gap.astype(jnp.bfloat16).reshape(members, capacity, vals),
        ],
        axis=1,
    )
    arrived = lax.all_to_all(sent, "blk", split_axis=0, concat_axis=0, tiled=True)
    return (
        arrived[:, : 2 * capacity].reshape(slot_count, vals),
        arrived[:, 2 * capacity :].reshape(slot_count // 2, vals),
    )


MESH = pl.DeviceIdType.MESH
CHUNKS = 4
COLS = 2
STRIP = 16


def hot_places(ids, owners, members, capacity):
    pairs, rows = owners.shape[1], ids.shape[1]
    iota = lax.broadcasted_iota
    ones = lambda mask: mask.astype(jnp.float32)
    narrow = lambda values: values.astype(jnp.bfloat16)
    dot = functools.partial(jnp.dot, preferred_element_type=jnp.float32)
    owner_hot = ones(iota(jnp.int32, (members, pairs), 0) == owners)
    after = ones(iota(jnp.int32, (pairs, pairs), 0) < iota(jnp.int32, (pairs, pairs), 1))
    counts = dot(narrow(owner_hot), narrow(after))
    place = owners.astype(jnp.float32) * capacity + jnp.sum(counts * owner_hot, axis=0, keepdims=True)
    pair_hot = ones(iota(jnp.int32, (pairs, rows), 0) == ids)
    after = ones(iota(jnp.int32, (rows, rows), 0) < iota(jnp.int32, (rows, rows), 1))
    earlier = dot(narrow(pair_hot), narrow(after))
    slot = dot(narrow(jnp.broadcast_to(place, (16, pairs))), narrow(pair_hot))[:1]
    second = jnp.sum(pair_hot * earlier, axis=0, keepdims=True)
    return slot, second


def kernel(
    members, capacity,
    train_ref, ids_hbm, owner_hbm, moment_hbm, val_hbm,
    influence_ref, gap_ref,
    ids_ref, owner_ref, moment_ref, val_ref, rows, pre, squares, held, hot, signed, outbox, inbox,
    row_sem, small_sem, z_send, x_send, y_send, d_send, c_send, held_sem, out_send, out_recv,
):
    depth = members // (2 * COLS)
    total, features = train_ref.shape
    vals = val_hbm.shape[0]
    wide = features // CHUNKS
    half = wide // 2
    slots = members * capacity
    me = lax.axis_index("blk")
    group = lax.axis_index("groups")
    core = lax.rem(me, 2)
    col = lax.rem(me // 2, COLS)
    layer = me // (2 * COLS)

    def at(dz, dx, dc=0):
        z = lax.rem(layer + dz, depth)
        x = lax.rem(col + dx, COLS)
        return (z * COLS + x) * 2 + lax.rem(core + dc, 2)

    aside = (group, at(0, 1))
    across = (1 - group, me)
    corner = (1 - group, at(0, 1))
    sibling = (group, at(0, 0, 1))

    smalls = []
    pairs = ((val_hbm, val_ref), (moment_hbm, moment_ref), (ids_hbm, ids_ref), (owner_hbm, owner_ref))
    for i, (source, target) in enumerate(pairs):
        copy = pltpu.make_async_copy(source, target, small_sem.at[i])
        copy.start()
        smalls.append(copy)
    fetches = []
    for k in range(CHUNKS):
        lanes = pl.ds(k * wide, wide)
        copy = pltpu.make_async_copy(train_ref.at[:, lanes], rows.at[:, lanes], row_sem.at[k])
        copy.start()
        fetches.append(copy)

    barrier = pltpu.get_barrier_semaphore()
    for step in range(1, members):
        pl.semaphore_signal(barrier, 1, device_id=(group, lax.rem(me + step, members)), device_id_type=MESH)
    pl.semaphore_signal(barrier, 1, device_id=across, device_id_type=MESH)
    pl.semaphore_signal(barrier, 1, device_id=corner, device_id_type=MESH)

    smalls[0].wait()
    val = val_ref[...].astype(jnp.float32)
    unit = val * lax.rsqrt(jnp.mean(val * val, axis=1, keepdims=True) + epsilon)
    for k in range(CHUNKS):
        both = [unit[:, k * wide + h * half : k * wide + (h + 1) * half] for h in range(2)]
        held[k, pl.ds(me, 1)] = jnp.concatenate(both, axis=0).astype(jnp.bfloat16)[None]
    pl.semaphore_wait(barrier, members + 1)

    sends = []

    def send(k, m, sem, to):
        copy = pltpu.make_async_remote_copy(
            src_ref=held.at[k, m], dst_ref=held.at[k, m], send_sem=sem, recv_sem=held_sem.at[k, m],
            device_id=to, device_id_type=MESH,
        )
        copy.start()
        sends.append(copy)

    def arrived(k, m):
        pltpu.make_async_remote_copy(
            src_ref=held.at[k, m], dst_ref=held.at[k, m], send_sem=out_send.at[0], recv_sem=held_sem.at[k, m],
            device_id=sibling, device_id_type=MESH,
        ).wait_recv()

    def to_core(k, dz, dx):
        send(k, at(dz, dx), c_send.at[k, dx * depth + dz], sibling)

    def to_side(k, dz):
        send(k, at(dz, 0), x_send.at[k, dz], aside)

    def to_group(k, dz):
        send(k, at(dz, 0), y_send.at[k, dz], across)

    def to_corner(k, dz):
        send(k, at(dz, 0), d_send.at[k, dz], corner)

    steps = range(1, depth)
    own = [2 * j + group for j in range(CHUNKS // 2)]
    other = [2 * j + 1 - group for j in range(CHUNKS // 2)]

    for j in range(CHUNKS // 2):
        for dz in steps:
            send(own[j], me, z_send.at[j, dz - 1], (group, at(dz, 0)))
        to_side(own[j], 0)
        to_side(other[j], 0)
        to_core(own[j], 0, 0)
        to_core(other[j], 0, 0)

    def from_z(j):
        for dz in steps:
            arrived(own[j], at(dz, 0))
            to_corner(own[j], dz)
            to_side(own[j], dz)
            to_group(own[j], dz)
            to_core(own[j], dz, 0)

    def side(j):
        arrived(other[j], at(0, 1))
        to_core(other[j], 0, 1)
        for dz in range(depth):
            arrived(own[j], at(dz, 1))
            to_core(own[j], dz, 1)

    def near(j):
        for dz in steps:
            arrived(other[j], at(dz, 0))
            to_core(other[j], dz, 0)

    def far(j):
        for dz in steps:
            arrived(other[j], at(dz, 1))
            to_core(other[j], dz, 1)

    def from_core(j):
        for k in (own[j], other[j]):
            for dz in range(depth):
                for dx in range(COLS):
                    arrived(k, at(dz, dx, 1))

    def scale(k):
        fetches[k].wait()
        lanes = pl.ds(k * wide, wide)

        def strip(i, _):
            band = pl.ds(pl.multiple_of(i * STRIP, STRIP), STRIP)
            scaled = (rows[band, lanes].astype(jnp.float32) * pre[:, lanes]).astype(jnp.bfloat16)
            rows[band, lanes] = scaled
            scaled = scaled.astype(jnp.float32)
            found = jnp.sum(scaled * scaled, axis=1, keepdims=True)
            squares[band, :] = found if k == 0 else squares[band, :] + found
            return 0

        lax.fori_loop(0, total // STRIP, strip, 0)

    def product(k):
        block = held[k].astype(jnp.float32)
        result = None
        for h in range(2):
            piece = block[:, h * vals : (h + 1) * vals].reshape(members * vals, half).astype(jnp.bfloat16)
            left = rows[:, pl.ds(k * wide + h * half, half)]
            term = lax.dot_general(left, piece, (((1,), (1,)), ((), ())), preferred_element_type=jnp.float32)
            result = term if result is None else result + term
        return result

    smalls[1].wait()
    pre[...] = 1.0 / (jnp.sqrt(moment_ref[...]) + 1e-08)
    scale(0)
    from_z(0)
    scale(1)
    from_z(1)
    side(0)
    near(0)
    scale(2)
    far(0)
    scale(3)
    side(1)
    near(1)
    smalls[2].wait()
    smalls[3].wait()
    slot, second = hot_places(ids_ref[...], owner_ref[...], members, capacity)
    place = lax.broadcasted_iota(jnp.int32, (2 * slots, total), 0).astype(jnp.float32)
    hot[...] = (place == 2 * slot + second).astype(jnp.float32).astype(jnp.bfloat16)
    place = lax.broadcasted_iota(jnp.int32, (slots, total), 0).astype(jnp.float32)
    signed[...] = jnp.where(place == slot, 1 - 2 * second, 0.0).astype(jnp.bfloat16)
    far(1)
    from_core(0)
    live = product(0) + product(1)
    from_core(1)
    live = live + product(2) + product(3)
    live = live * (lax.rsqrt(squares[...] / features + epsilon) / math.sqrt(features))

    high = live.astype(jnp.bfloat16)
    low = (live - high.astype(jnp.float32)).astype(jnp.bfloat16)
    influence = jnp.dot(hot[...], high, preferred_element_type=jnp.float32)
    gap = jnp.dot(signed[...], high, preferred_element_type=jnp.float32)
    gap = gap + jnp.dot(signed[...], low, preferred_element_type=jnp.float32)
    outbox[:, : 2 * capacity] = influence.astype(jnp.bfloat16).reshape(members, 2 * capacity, -1)
    outbox[:, 2 * capacity :] = gap.astype(jnp.bfloat16).reshape(members, capacity, -1)

    for step in range(1, members):
        to = lax.rem(me + step, members)
        copy = pltpu.make_async_remote_copy(
            src_ref=outbox.at[to], dst_ref=inbox.at[me], send_sem=out_send.at[step], recv_sem=out_recv.at[me],
            device_id=(group, to), device_id_type=MESH,
        )
        copy.start()
        sends.append(copy)

    def place_block(m, ref):
        influence_ref[pl.ds(pl.multiple_of(m * 2 * capacity, 2 * capacity), 2 * capacity), :] = ref[m, : 2 * capacity]
        gap_ref[pl.ds(pl.multiple_of(m * capacity, capacity), capacity), :] = ref[m, 2 * capacity :]

    place_block(me, outbox)
    for step in range(1, members):
        m = lax.rem(me + members - step, members)
        pltpu.make_async_remote_copy(
            src_ref=outbox.at[m], dst_ref=inbox.at[m], send_sem=out_send.at[0], recv_sem=out_recv.at[m],
            device_id=sibling, device_id_type=MESH,
        ).wait_recv()
        place_block(m, inbox)
    for copy in sends:
        copy.wait_send()


def on_device(train_rows, pair_ids, pair_owner, second_moment, val_rows):
    members = lax.axis_size("blk")
    total, features = train_rows.shape
    capacity = max(2, total // members)
    vals = val_rows.shape[0]
    if capacity % 16 or members % (2 * COLS) or lax.axis_size("groups") != 2:
        return plain(train_rows, pair_ids, pair_owner, second_moment, val_rows)
    slots, width, wide = members * capacity, members * vals, features // CHUNKS
    depth = members // (2 * COLS)
    vmem = pl.BlockSpec(memory_space=pltpu.VMEM)
    dma = pltpu.SemaphoreType.DMA
    return pl.pallas_call(
        functools.partial(kernel, members, capacity),
        out_shape=(
            jax.ShapeDtypeStruct((2 * slots, width), jnp.bfloat16),
            jax.ShapeDtypeStruct((slots, width), jnp.bfloat16),
        ),
        in_specs=[pl.BlockSpec(memory_space=pltpu.HBM)] * 5,
        out_specs=(vmem, vmem),
        scratch_shapes=[
            pltpu.VMEM((1, total), jnp.int32),
            pltpu.VMEM((1, total // 2), jnp.int32),
            pltpu.VMEM((1, features), jnp.float32),
            pltpu.VMEM((vals, features), jnp.bfloat16),
            pltpu.VMEM((total, features), jnp.bfloat16),
            pltpu.VMEM((1, features), jnp.float32),
            pltpu.VMEM((total, 1), jnp.float32),
            pltpu.VMEM((CHUNKS, members, 2 * vals, wide // 2), jnp.bfloat16),
            pltpu.VMEM((2 * slots, total), jnp.bfloat16),
            pltpu.VMEM((slots, total), jnp.bfloat16),
            pltpu.VMEM((members, 3 * capacity, width), jnp.bfloat16),
            pltpu.VMEM((members, 3 * capacity, width), jnp.bfloat16),
            dma((CHUNKS,)),
            dma((4,)),
            dma((CHUNKS // 2, depth)),
            dma((CHUNKS, depth)),
            dma((CHUNKS, depth)),
            dma((CHUNKS, COLS * depth)),
            dma((CHUNKS, COLS * depth)),
            dma((CHUNKS, members)),
            dma((members,)),
            dma((members,)),
        ],
        compiler_params=pltpu.CompilerParams(
            collective_id=0, has_side_effects=True, vmem_limit_bytes=64 * 2**20
        ),
        cost_estimate=pl.CostEstimate(
            flops=2 * total * features * width, bytes_accessed=2 * total * features, transcendentals=0
        ),
    )(train_rows, pair_ids.reshape(1, total), pair_owner.reshape(1, total // 2), second_moment.reshape(1, features), val_rows)


def solution(mesh):
    return jax.shard_map(
        on_device,
        mesh=mesh,
        in_specs=(
            P(("groups", "blk"), None),
            P(("groups", "blk")),
            P(("groups", "blk"), None),
            P(),
            P("blk", None),
        ),
        out_specs=(P(("groups", "blk"), None), P(("groups", "blk"), None)),
        check_vma=False,
    )
```

```python
import functools
import math

import jax
import jax.numpy as jnp
from jax import lax
from jax.experimental import pallas as pl
from jax.experimental.pallas import tpu as pltpu
from jax.sharding import PartitionSpec as P

epsilon = 1e-05


def unit_rows(rows):
    wide = rows.astype(jnp.float32)
    return (wide * lax.rsqrt(jnp.mean(wide * wide, axis=1, keepdims=True) + epsilon)).astype(
        jnp.bfloat16
    )


def plain(train_rows, pair_ids, pair_owner, second_moment, val_rows):
    members = lax.axis_size("blk")
    row_total, features = train_rows.shape
    pair_total = row_total // 2
    capacity = max(2, 2 * pair_total // members)
    gathered = lax.all_gather(unit_rows(val_rows), "blk", axis=0, tiled=True)
    vals = gathered.shape[0]
    owner_hot = (pair_owner == jnp.arange(members, dtype=jnp.int32)[None, :]).astype(jnp.float32)
    before = jnp.tri(pair_total, k=-1, dtype=jnp.float32)
    position = jnp.sum(jnp.dot(before, owner_hot) * owner_hot, axis=1, keepdims=True)
    place = pair_owner.astype(jnp.float32) * (2 * capacity) + 2 * position
    pair_hot = (jnp.arange(pair_total, dtype=jnp.int32)[:, None] == pair_ids[None, :]).astype(jnp.float32)
    earlier = jnp.dot(pair_hot, jnp.tri(row_total, k=-1, dtype=jnp.float32).T)
    target = jnp.sum(pair_hot * (place + earlier), axis=0).astype(jnp.int32)
    slot_count = members * 2 * capacity
    hot = (jnp.arange(slot_count, dtype=jnp.int32)[:, None] == target[None, :]).astype(jnp.bfloat16)
    precondition = 1.0 / (jnp.sqrt(second_moment) + 1e-08)
    scaled = (train_rows.astype(jnp.float32) * precondition[None, :]).astype(jnp.bfloat16)
    live = lax.dot_general(
        unit_rows(scaled), gathered, (((1,), (1,)), ((), ())), preferred_element_type=jnp.float32
    ) / math.sqrt(features)
    high = live.astype(jnp.bfloat16)
    low = (live - high.astype(jnp.float32)).astype(jnp.bfloat16)
    influence = jnp.dot(hot, high, preferred_element_type=jnp.float32)
    rest = jnp.dot(hot, low, preferred_element_type=jnp.float32)
    paired = (influence + rest).reshape(-1, 2, vals)
    gap = paired[:, 0] - paired[:, 1]
    sent = jnp.concatenate(
        [
            influence.astype(jnp.bfloat16).reshape(members, 2 * capacity, vals),
            gap.astype(jnp.bfloat16).reshape(members, capacity, vals),
        ],
        axis=1,
    )
    arrived = lax.all_to_all(sent, "blk", split_axis=0, concat_axis=0, tiled=True)
    return (
        arrived[:, : 2 * capacity].reshape(slot_count, vals),
        arrived[:, 2 * capacity :].reshape(slot_count // 2, vals),
    )


MESH = pl.DeviceIdType.MESH
CHUNKS = 4
COLS = 2
STRIP = 16


def hot_places(ids, owners, members, capacity):
    pairs, rows = owners.shape[1], ids.shape[1]
    iota = lax.broadcasted_iota
    ones = lambda mask: mask.astype(jnp.float32)
    narrow = lambda values: values.astype(jnp.bfloat16)
    dot = functools.partial(jnp.dot, preferred_element_type=jnp.float32)
    owner_hot = ones(iota(jnp.int32, (members, pairs), 0) == owners)
    after = ones(iota(jnp.int32, (pairs, pairs), 0) < iota(jnp.int32, (pairs, pairs), 1))
    counts = dot(narrow(owner_hot), narrow(after))
    place = owners.astype(jnp.float32) * capacity + jnp.sum(counts * owner_hot, axis=0, keepdims=True)
    pair_hot = ones(iota(jnp.int32, (pairs, rows), 0) == ids)
    after = ones(iota(jnp.int32, (rows, rows), 0) < iota(jnp.int32, (rows, rows), 1))
    earlier = dot(narrow(pair_hot), narrow(after))
    slot = dot(narrow(jnp.broadcast_to(place, (16, pairs))), narrow(pair_hot))[:1]
    second = jnp.sum(pair_hot * earlier, axis=0, keepdims=True)
    return slot, second


def kernel(
    members, capacity,
    train_ref, ids_hbm, owner_hbm, moment_hbm, val_hbm,
    inbox,
    ids_ref, owner_ref, moment_ref, val_ref, rows, pre, squares, held, hot, signed, outbox,
    row_sem, small_sem, z_send, x_send, y_send, d_send, c_send, held_sem, core_sem, out_send, out_recv,
):
    depth = members // (2 * COLS)
    total, features = train_ref.shape
    vals = val_hbm.shape[0]
    wide = features // CHUNKS
    half = wide // 2
    slots = members * capacity
    me = lax.axis_index("blk")
    group = lax.axis_index("groups")
    core = lax.rem(me, 2)
    col = lax.rem(me // 2, COLS)
    layer = me // (2 * COLS)

    def at(dz, dx, dc=0):
        z = lax.rem(layer + dz, depth)
        x = lax.rem(col + dx, COLS)
        return (z * COLS + x) * 2 + lax.rem(core + dc, 2)

    aside = (group, at(0, 1))
    across = (1 - group, me)

    def slab(dz, dx):
        return (core * COLS + lax.rem(col + dx, COLS)) * depth + lax.rem(layer + dz, depth)

    corner = (1 - group, at(0, 1))
    sibling = (group, at(0, 0, 1))

    smalls = []
    pairs = ((val_hbm, val_ref), (moment_hbm, moment_ref), (ids_hbm, ids_ref), (owner_hbm, owner_ref))
    for i, (source, target) in enumerate(pairs):
        copy = pltpu.make_async_copy(source, target, small_sem.at[i])
        copy.start()
        smalls.append(copy)
    fetches = []
    for k in range(CHUNKS):
        lanes = pl.ds(k * wide, wide)
        copy = pltpu.make_async_copy(train_ref.at[:, lanes], rows.at[:, lanes], row_sem.at[k])
        copy.start()
        fetches.append(copy)

    barrier = pltpu.get_barrier_semaphore()
    for step in range(1, members):
        pl.semaphore_signal(barrier, 1, device_id=(group, lax.rem(me + step, members)), device_id_type=MESH)
    pl.semaphore_signal(barrier, 1, device_id=across, device_id_type=MESH)
    pl.semaphore_signal(barrier, 1, device_id=corner, device_id_type=MESH)

    smalls[0].wait()
    val = val_ref[...].astype(jnp.float32)
    unit = val * lax.rsqrt(jnp.mean(val * val, axis=1, keepdims=True) + epsilon)
    for k in range(CHUNKS):
        both = [unit[:, k * wide + h * half : k * wide + (h + 1) * half] for h in range(2)]
        held[k, pl.ds(slab(0, 0), 1)] = jnp.concatenate(both, axis=0).astype(jnp.bfloat16)[None]
    pl.semaphore_wait(barrier, members + 1)

    sends = []

    def send(k, m, sem, to):
        copy = pltpu.make_async_remote_copy(
            src_ref=held.at[k, m], dst_ref=held.at[k, m], send_sem=sem, recv_sem=held_sem.at[k, m],
            device_id=to, device_id_type=MESH,
        )
        copy.start()
        sends.append(copy)

    def arrived(k, m):
        pltpu.make_async_remote_copy(
            src_ref=held.at[k, m], dst_ref=held.at[k, m], send_sem=out_send.at[0], recv_sem=held_sem.at[k, m],
            device_id=sibling, device_id_type=MESH,
        ).wait_recv()

    def core_copy(k, which, x):
        block = held.at[k, pl.ds((which * COLS + x) * depth, depth)]
        return pltpu.make_async_remote_copy(
            src_ref=block, dst_ref=block, send_sem=c_send.at[k, x], recv_sem=core_sem.at[k, x],
            device_id=sibling, device_id_type=MESH,
        )

    def to_core(k, dx):
        copy = core_copy(k, core, lax.rem(col + dx, COLS))
        copy.start()
        sends.append(copy)

    def to_side(k, dz):
        send(k, slab(dz, 0), x_send.at[k, dz], aside)

    def to_group(k, dz):
        send(k, slab(dz, 0), y_send.at[k, dz], across)

    def to_corner(k, dz):
        send(k, slab(dz, 0), d_send.at[k, dz], corner)

    steps = range(1, depth)
    own = [2 * j + group for j in range(CHUNKS // 2)]
    other = [2 * j + 1 - group for j in range(CHUNKS // 2)]

    for j in range(CHUNKS // 2):
        for dz in steps:
            send(own[j], slab(0, 0), z_send.at[j, dz - 1], (group, at(dz, 0)))
        to_side(own[j], 0)
        to_side(other[j], 0)

    def from_z(j):
        for dz in steps:
            arrived(own[j], slab(dz, 0))
            to_corner(own[j], dz)
            to_side(own[j], dz)
            to_group(own[j], dz)
        to_core(own[j], 0)

    def side(j):
        arrived(other[j], slab(0, 1))
        for dz in range(depth):
            arrived(own[j], slab(dz, 1))
        to_core(own[j], 1)

    def near(j):
        for dz in steps:
            arrived(other[j], slab(dz, 0))
        to_core(other[j], 0)

    def far(j):
        for dz in steps:
            arrived(other[j], slab(dz, 1))
        to_core(other[j], 1)

    def from_core(j):
        for k in (own[j], other[j]):
            for x in range(COLS):
                core_copy(k, 1 - core, x).wait_recv()

    def scale(k):
        fetches[k].wait()
        lanes = pl.ds(k * wide, wide)

        def strip(i, _):
            band = pl.ds(pl.multiple_of(i * STRIP, STRIP), STRIP)
            scaled = (rows[band, lanes].astype(jnp.float32) * pre[:, lanes]).astype(jnp.bfloat16)
            rows[band, lanes] = scaled
            scaled = scaled.astype(jnp.float32)
            found = jnp.sum(scaled * scaled, axis=1, keepdims=True)
            squares[band, :] = found if k == 0 else squares[band, :] + found
            return 0

        lax.fori_loop(0, total // STRIP, strip, 0)

    def product(k):
        order = [(m % 2 * COLS + m // 2 % COLS) * depth + m // (2 * COLS) for m in range(members)]
        block = jnp.stack([held[k, i] for i in order]).astype(jnp.float32)
        result = None
        for h in range(2):
            piece = block[:, h * vals : (h + 1) * vals].reshape(members * vals, half).astype(jnp.bfloat16)
            left = rows[:, pl.ds(k * wide + h * half, half)]
            term = lax.dot_general(left, piece, (((1,), (1,)), ((), ())), preferred_element_type=jnp.float32)
            result = term if result is None else result + term
        return result

    smalls[1].wait()
    pre[...] = 1.0 / (jnp.sqrt(moment_ref[...]) + 1e-08)
    scale(0)
    from_z(0)
    scale(1)
    from_z(1)
    side(0)
    near(0)
    scale(2)
    far(0)
    scale(3)
    side(1)
    near(1)
    smalls[2].wait()
    smalls[3].wait()
    slot, second = hot_places(ids_ref[...], owner_ref[...], members, capacity)
    place = lax.broadcasted_iota(jnp.int32, (2 * slots, total), 0).astype(jnp.float32)
    hot[...] = (place == 2 * slot + second).astype(jnp.float32).astype(jnp.bfloat16)
    place = lax.broadcasted_iota(jnp.int32, (slots, total), 0).astype(jnp.float32)
    signed[...] = jnp.where(place == slot, 1 - 2 * second, 0.0).astype(jnp.bfloat16)
    far(1)
    from_core(0)
    live = product(0) + product(1)
    from_core(1)
    live = live + product(2) + product(3)
    live = live * (lax.rsqrt(squares[...] / features + epsilon) / math.sqrt(features))

    high = live.astype(jnp.bfloat16)
    low = (live - high.astype(jnp.float32)).astype(jnp.bfloat16)
    influence = jnp.dot(hot[...], high, preferred_element_type=jnp.float32)
    gap = jnp.dot(signed[...], high, preferred_element_type=jnp.float32)
    gap = gap + jnp.dot(signed[...], low, preferred_element_type=jnp.float32)
    outbox[:, : 2 * capacity] = influence.astype(jnp.bfloat16).reshape(members, 2 * capacity, -1)
    outbox[:, 2 * capacity :] = gap.astype(jnp.bfloat16).reshape(members, capacity, -1)

    for step in range(1, members):
        to = lax.rem(me + step, members)
        copy = pltpu.make_async_remote_copy(
            src_ref=outbox.at[to], dst_ref=inbox.at[me], send_sem=out_send.at[step], recv_sem=out_recv.at[me],
            device_id=(group, to), device_id_type=MESH,
        )
        copy.start()
        sends.append(copy)

    kept = pltpu.make_async_copy(outbox.at[me], inbox.at[me], out_send.at[0])
    kept.start()
    for step in range(1, members):
        m = lax.rem(me + members - step, members)
        pltpu.make_async_remote_copy(
            src_ref=outbox.at[m], dst_ref=inbox.at[m], send_sem=out_send.at[0], recv_sem=out_recv.at[m],
            device_id=sibling, device_id_type=MESH,
        ).wait_recv()
    kept.wait()
    for copy in sends:
        copy.wait_send()


def on_device(train_rows, pair_ids, pair_owner, second_moment, val_rows):
    members = lax.axis_size("blk")
    total, features = train_rows.shape
    capacity = max(2, total // members)
    vals = val_rows.shape[0]
    if capacity % 16 or members % (2 * COLS) or lax.axis_size("groups") != 2:
        return plain(train_rows, pair_ids, pair_owner, second_moment, val_rows)
    slots, width, wide = members * capacity, members * vals, features // CHUNKS
    depth = members // (2 * COLS)
    dma = pltpu.SemaphoreType.DMA
    arrived = pl.pallas_call(
        functools.partial(kernel, members, capacity),
        out_shape=jax.ShapeDtypeStruct((members, 3 * capacity, width), jnp.bfloat16),
        in_specs=[pl.BlockSpec(memory_space=pltpu.HBM)] * 5,
        out_specs=pl.BlockSpec(memory_space=pltpu.HBM),
        scratch_shapes=[
            pltpu.VMEM((1, total), jnp.int32),
            pltpu.VMEM((1, total // 2), jnp.int32),
            pltpu.VMEM((1, features), jnp.float32),
            pltpu.VMEM((vals, features), jnp.bfloat16),
            pltpu.VMEM((total, features), jnp.bfloat16),
            pltpu.VMEM((1, features), jnp.float32),
            pltpu.VMEM((total, 1), jnp.float32),
            pltpu.VMEM((CHUNKS, members, 2 * vals, wide // 2), jnp.bfloat16),
            pltpu.VMEM((2 * slots, total), jnp.bfloat16),
            pltpu.VMEM((slots, total), jnp.bfloat16),
            pltpu.VMEM((members, 3 * capacity, width), jnp.bfloat16),
            dma((CHUNKS,)),
            dma((4,)),
            dma((CHUNKS // 2, depth)),
            dma((CHUNKS, depth)),
            dma((CHUNKS, depth)),
            dma((CHUNKS, depth)),
            dma((CHUNKS, COLS)),
            dma((CHUNKS, members)),
            dma((CHUNKS, COLS)),
            dma((members,)),
            dma((members,)),
        ],
        compiler_params=pltpu.CompilerParams(
            collective_id=0, has_side_effects=True, vmem_limit_bytes=64 * 2**20
        ),
        cost_estimate=pl.CostEstimate(
            flops=2 * total * features * width, bytes_accessed=2 * total * features, transcendentals=0
        ),
    )(train_rows, pair_ids.reshape(1, total), pair_owner.reshape(1, total // 2), second_moment.reshape(1, features), val_rows)
    return (
        arrived[:, : 2 * capacity].reshape(2 * slots, width),
        arrived[:, 2 * capacity :].reshape(slots, width),
    )


def solution(mesh):
    return jax.shard_map(
        on_device,
        mesh=mesh,
        in_specs=(
            P(("groups", "blk"), None),
            P(("groups", "blk")),
            P(("groups", "blk"), None),
            P(),
            P("blk", None),
        ),
        out_specs=(P(("groups", "blk"), None), P(("groups", "blk"), None)),
        check_vma=False,
    )
```

```python
import functools
import math

import jax
import jax.numpy as jnp
from jax import lax
from jax.experimental import pallas as pl
from jax.experimental.pallas import tpu as pltpu
from jax.sharding import PartitionSpec as P

epsilon = 1e-05


def unit_rows(rows):
    wide = rows.astype(jnp.float32)
    return (wide * lax.rsqrt(jnp.mean(wide * wide, axis=1, keepdims=True) + epsilon)).astype(
        jnp.bfloat16
    )


def plain(train_rows, pair_ids, pair_owner, second_moment, val_rows):
    members = lax.axis_size("blk")
    row_total, features = train_rows.shape
    pair_total = row_total // 2
    capacity = max(2, 2 * pair_total // members)
    gathered = lax.all_gather(unit_rows(val_rows), "blk", axis=0, tiled=True)
    vals = gathered.shape[0]
    owner_hot = (pair_owner == jnp.arange(members, dtype=jnp.int32)[None, :]).astype(jnp.float32)
    before = jnp.tri(pair_total, k=-1, dtype=jnp.float32)
    position = jnp.sum(jnp.dot(before, owner_hot) * owner_hot, axis=1, keepdims=True)
    place = pair_owner.astype(jnp.float32) * (2 * capacity) + 2 * position
    pair_hot = (jnp.arange(pair_total, dtype=jnp.int32)[:, None] == pair_ids[None, :]).astype(jnp.float32)
    earlier = jnp.dot(pair_hot, jnp.tri(row_total, k=-1, dtype=jnp.float32).T)
    target = jnp.sum(pair_hot * (place + earlier), axis=0).astype(jnp.int32)
    slot_count = members * 2 * capacity
    hot = (jnp.arange(slot_count, dtype=jnp.int32)[:, None] == target[None, :]).astype(jnp.bfloat16)
    precondition = 1.0 / (jnp.sqrt(second_moment) + 1e-08)
    scaled = (train_rows.astype(jnp.float32) * precondition[None, :]).astype(jnp.bfloat16)
    live = lax.dot_general(
        unit_rows(scaled), gathered, (((1,), (1,)), ((), ())), preferred_element_type=jnp.float32
    ) / math.sqrt(features)
    high = live.astype(jnp.bfloat16)
    low = (live - high.astype(jnp.float32)).astype(jnp.bfloat16)
    influence = jnp.dot(hot, high, preferred_element_type=jnp.float32)
    rest = jnp.dot(hot, low, preferred_element_type=jnp.float32)
    paired = (influence + rest).reshape(-1, 2, vals)
    gap = paired[:, 0] - paired[:, 1]
    sent = jnp.concatenate(
        [
            influence.astype(jnp.bfloat16).reshape(members, 2 * capacity, vals),
            gap.astype(jnp.bfloat16).reshape(members, capacity, vals),
        ],
        axis=1,
    )
    arrived = lax.all_to_all(sent, "blk", split_axis=0, concat_axis=0, tiled=True)
    return (
        arrived[:, : 2 * capacity].reshape(slot_count, vals),
        arrived[:, 2 * capacity :].reshape(slot_count // 2, vals),
    )


MESH = pl.DeviceIdType.MESH
CHUNKS = 4
COLS = 2
STRIP = 16


def hot_places(ids, owners, members, capacity):
    pairs, rows = owners.shape[1], ids.shape[1]
    iota = lax.broadcasted_iota
    ones = lambda mask: mask.astype(jnp.float32)
    narrow = lambda values: values.astype(jnp.bfloat16)
    dot = functools.partial(jnp.dot, preferred_element_type=jnp.float32)
    owner_hot = ones(iota(jnp.int32, (members, pairs), 0) == owners)
    after = ones(iota(jnp.int32, (pairs, pairs), 0) < iota(jnp.int32, (pairs, pairs), 1))
    counts = dot(narrow(owner_hot), narrow(after))
    place = owners.astype(jnp.float32) * capacity + jnp.sum(counts * owner_hot, axis=0, keepdims=True)
    pair_hot = ones(iota(jnp.int32, (pairs, rows), 0) == ids)
    after = ones(iota(jnp.int32, (rows, rows), 0) < iota(jnp.int32, (rows, rows), 1))
    earlier = dot(narrow(pair_hot), narrow(after))
    slot = dot(narrow(jnp.broadcast_to(place, (16, pairs))), narrow(pair_hot))[:1]
    second = jnp.sum(pair_hot * earlier, axis=0, keepdims=True)
    return slot, second


def kernel(
    members, capacity,
    train_ref, ids_hbm, owner_hbm, moment_hbm, val_hbm,
    inbox,
    ids_ref, owner_ref, moment_ref, val_ref, rows, pre, squares, held, hot, signed, outbox,
    row_sem, small_sem, z_send, x_send, y_send, d_send, c_send, held_sem, core_sem, out_send, out_recv,
):
    depth = members // (2 * COLS)
    total, features = train_ref.shape
    vals = val_hbm.shape[0]
    wide = features // CHUNKS
    half = wide // 2
    slots = members * capacity
    me = lax.axis_index("blk")
    group = lax.axis_index("groups")
    core = lax.rem(me, 2)
    col = lax.rem(me // 2, COLS)
    layer = me // (2 * COLS)

    def at(dz, dx, dc=0):
        z = lax.rem(layer + dz, depth)
        x = lax.rem(col + dx, COLS)
        return (z * COLS + x) * 2 + lax.rem(core + dc, 2)

    aside = (group, at(0, 1))
    across = (1 - group, me)

    def slab(dz, dx):
        return (core * COLS + lax.rem(col + dx, COLS)) * depth + lax.rem(layer + dz, depth)

    corner = (1 - group, at(0, 1))
    sibling = (group, at(0, 0, 1))

    smalls = []
    pairs = ((val_hbm, val_ref), (moment_hbm, moment_ref), (ids_hbm, ids_ref), (owner_hbm, owner_ref))
    for i, (source, target) in enumerate(pairs):
        copy = pltpu.make_async_copy(source, target, small_sem.at[i])
        copy.start()
        smalls.append(copy)
    fetches = []
    for k in range(CHUNKS):
        lanes = pl.ds(k * wide, wide)
        copy = pltpu.make_async_copy(train_ref.at[:, lanes], rows.at[:, lanes], row_sem.at[k])
        copy.start()
        fetches.append(copy)

    barrier = pltpu.get_barrier_semaphore()
    for step in range(1, members):
        pl.semaphore_signal(barrier, 1, device_id=(group, lax.rem(me + step, members)), device_id_type=MESH)
    pl.semaphore_signal(barrier, 1, device_id=across, device_id_type=MESH)
    pl.semaphore_signal(barrier, 1, device_id=corner, device_id_type=MESH)

    smalls[0].wait()
    val = val_ref[...].astype(jnp.float32)
    unit = val * lax.rsqrt(jnp.mean(val * val, axis=1, keepdims=True) + epsilon)
    for k in range(CHUNKS):
        both = [unit[:, k * wide + h * half : k * wide + (h + 1) * half] for h in range(2)]
        held[k, pl.ds(slab(0, 0), 1)] = jnp.concatenate(both, axis=0).astype(jnp.bfloat16)[None]
    pl.semaphore_wait(barrier, members + 1)

    sends = []

    def send(k, m, sem, to):
        copy = pltpu.make_async_remote_copy(
            src_ref=held.at[k, m], dst_ref=held.at[k, m], send_sem=sem, recv_sem=held_sem.at[k, m],
            device_id=to, device_id_type=MESH,
        )
        copy.start()
        sends.append(copy)

    def arrived(k, m):
        pltpu.make_async_remote_copy(
            src_ref=held.at[k, m], dst_ref=held.at[k, m], send_sem=out_send.at[0], recv_sem=held_sem.at[k, m],
            device_id=sibling, device_id_type=MESH,
        ).wait_recv()

    def core_copy(k, which, x):
        block = held.at[k, pl.ds((which * COLS + x) * depth, depth)]
        return pltpu.make_async_remote_copy(
            src_ref=block, dst_ref=block, send_sem=c_send.at[k, x], recv_sem=core_sem.at[k, x],
            device_id=sibling, device_id_type=MESH,
        )

    def to_core(k, dx):
        copy = core_copy(k, core, lax.rem(col + dx, COLS))
        copy.start()
        sends.append(copy)

    def to_side(k, dz):
        send(k, slab(dz, 0), x_send.at[k, dz], aside)

    def to_group(k, dz):
        send(k, slab(dz, 0), y_send.at[k, dz], across)

    def to_corner(k, dz):
        send(k, slab(dz, 0), d_send.at[k, dz], corner)

    steps = range(1, depth)
    own = [2 * j + group for j in range(CHUNKS // 2)]
    other = [2 * j + 1 - group for j in range(CHUNKS // 2)]

    for j in range(CHUNKS // 2):
        for dz in steps:
            send(own[j], slab(0, 0), z_send.at[j, dz - 1], (group, at(dz, 0)))
        to_side(own[j], 0)
        to_side(other[j], 0)

    def from_z(j):
        for dz in steps:
            arrived(own[j], slab(dz, 0))
            to_corner(own[j], dz)
            to_side(own[j], dz)
            to_group(own[j], dz)
        to_core(own[j], 0)

    def side(j):
        arrived(other[j], slab(0, 1))
        for dz in range(depth):
            arrived(own[j], slab(dz, 1))
        to_core(own[j], 1)

    def near(j):
        for dz in steps:
            arrived(other[j], slab(dz, 0))
        to_core(other[j], 0)

    def far(j):
        for dz in steps:
            arrived(other[j], slab(dz, 1))
        to_core(other[j], 1)

    def from_core(j):
        for k in (own[j], other[j]):
            for x in range(COLS):
                core_copy(k, 1 - core, x).wait_recv()

    def scale(k):
        fetches[k].wait()
        lanes = pl.ds(k * wide, wide)

        def strip(i, _):
            band = pl.ds(pl.multiple_of(i * STRIP, STRIP), STRIP)
            scaled = (rows[band, lanes].astype(jnp.float32) * pre[:, lanes]).astype(jnp.bfloat16)
            rows[band, lanes] = scaled
            scaled = scaled.astype(jnp.float32)
            found = jnp.sum(scaled * scaled, axis=1, keepdims=True)
            squares[band, :] = found if k == 0 else squares[band, :] + found
            return 0

        lax.fori_loop(0, total // STRIP, strip, 0)

    def product(k):
        order = [(m % 2 * COLS + m // 2 % COLS) * depth + m // (2 * COLS) for m in range(members)]
        block = jnp.stack([held[k, i] for i in order]).astype(jnp.float32)
        result = None
        for h in range(2):
            piece = block[:, h * vals : (h + 1) * vals].reshape(members * vals, half).astype(jnp.bfloat16)
            left = rows[:, pl.ds(k * wide + h * half, half)]
            term = lax.dot_general(left, piece, (((1,), (1,)), ((), ())), preferred_element_type=jnp.float32)
            result = term if result is None else result + term
        return result

    smalls[1].wait()
    pre[...] = 1.0 / (jnp.sqrt(moment_ref[...]) + 1e-08)
    smalls[2].wait()
    smalls[3].wait()
    slot, second = hot_places(ids_ref[...], owner_ref[...], members, capacity)
    place = lax.broadcasted_iota(jnp.int32, (2 * slots, total), 0).astype(jnp.float32)
    hot[...] = (place == 2 * slot + second).astype(jnp.float32).astype(jnp.bfloat16)
    place = lax.broadcasted_iota(jnp.int32, (slots, total), 0).astype(jnp.float32)
    signed[...] = jnp.where(place == slot, 1 - 2 * second, 0.0).astype(jnp.bfloat16)
    scale(0)
    from_z(0)
    scale(1)
    from_z(1)
    side(0)
    near(0)
    scale(2)
    far(0)
    scale(3)
    side(1)
    near(1)
    far(1)
    from_core(0)
    live = product(0) + product(1)
    from_core(1)
    live = live + product(2) + product(3)
    live = live * (lax.rsqrt(squares[...] / features + epsilon) / math.sqrt(features))

    high = live.astype(jnp.bfloat16)
    low = (live - high.astype(jnp.float32)).astype(jnp.bfloat16)
    influence = jnp.dot(hot[...], high, preferred_element_type=jnp.float32)
    gap = jnp.dot(signed[...], high, preferred_element_type=jnp.float32)
    gap = gap + jnp.dot(signed[...], low, preferred_element_type=jnp.float32)
    outbox[:, : 2 * capacity] = influence.astype(jnp.bfloat16).reshape(members, 2 * capacity, -1)
    outbox[:, 2 * capacity :] = gap.astype(jnp.bfloat16).reshape(members, capacity, -1)

    for step in range(1, members):
        to = lax.rem(me + step, members)
        copy = pltpu.make_async_remote_copy(
            src_ref=outbox.at[to], dst_ref=inbox.at[me], send_sem=out_send.at[step], recv_sem=out_recv.at[me],
            device_id=(group, to), device_id_type=MESH,
        )
        copy.start()
        sends.append(copy)

    kept = pltpu.make_async_copy(outbox.at[me], inbox.at[me], out_send.at[0])
    kept.start()
    for step in range(1, members):
        m = lax.rem(me + members - step, members)
        pltpu.make_async_remote_copy(
            src_ref=outbox.at[m], dst_ref=inbox.at[m], send_sem=out_send.at[0], recv_sem=out_recv.at[m],
            device_id=sibling, device_id_type=MESH,
        ).wait_recv()
    kept.wait()
    for copy in sends:
        copy.wait_send()


def on_device(train_rows, pair_ids, pair_owner, second_moment, val_rows):
    members = lax.axis_size("blk")
    total, features = train_rows.shape
    capacity = max(2, total // members)
    vals = val_rows.shape[0]
    if capacity % 16 or members % (2 * COLS) or lax.axis_size("groups") != 2:
        return plain(train_rows, pair_ids, pair_owner, second_moment, val_rows)
    slots, width, wide = members * capacity, members * vals, features // CHUNKS
    depth = members // (2 * COLS)
    dma = pltpu.SemaphoreType.DMA
    arrived = pl.pallas_call(
        functools.partial(kernel, members, capacity),
        out_shape=jax.ShapeDtypeStruct((members, 3 * capacity, width), jnp.bfloat16),
        in_specs=[pl.BlockSpec(memory_space=pltpu.HBM)] * 5,
        out_specs=pl.BlockSpec(memory_space=pltpu.HBM),
        scratch_shapes=[
            pltpu.VMEM((1, total), jnp.int32),
            pltpu.VMEM((1, total // 2), jnp.int32),
            pltpu.VMEM((1, features), jnp.float32),
            pltpu.VMEM((vals, features), jnp.bfloat16),
            pltpu.VMEM((total, features), jnp.bfloat16),
            pltpu.VMEM((1, features), jnp.float32),
            pltpu.VMEM((total, 1), jnp.float32),
            pltpu.VMEM((CHUNKS, members, 2 * vals, wide // 2), jnp.bfloat16),
            pltpu.VMEM((2 * slots, total), jnp.bfloat16),
            pltpu.VMEM((slots, total), jnp.bfloat16),
            pltpu.VMEM((members, 3 * capacity, width), jnp.bfloat16),
            dma((CHUNKS,)),
            dma((4,)),
            dma((CHUNKS // 2, depth)),
            dma((CHUNKS, depth)),
            dma((CHUNKS, depth)),
            dma((CHUNKS, depth)),
            dma((CHUNKS, COLS)),
            dma((CHUNKS, members)),
            dma((CHUNKS, COLS)),
            dma((members,)),
            dma((members,)),
        ],
        compiler_params=pltpu.CompilerParams(
            collective_id=0, has_side_effects=True, vmem_limit_bytes=64 * 2**20
        ),
        cost_estimate=pl.CostEstimate(
            flops=2 * total * features * width, bytes_accessed=2 * total * features, transcendentals=0
        ),
    )(train_rows, pair_ids.reshape(1, total), pair_owner.reshape(1, total // 2), second_moment.reshape(1, features), val_rows)
    return (
        arrived[:, : 2 * capacity].reshape(2 * slots, width),
        arrived[:, 2 * capacity :].reshape(slots, width),
    )


def solution(mesh):
    return jax.shard_map(
        on_device,
        mesh=mesh,
        in_specs=(
            P(("groups", "blk"), None),
            P(("groups", "blk")),
            P(("groups", "blk"), None),
            P(),
            P("blk", None),
        ),
        out_specs=(P(("groups", "blk"), None), P(("groups", "blk"), None)),
        check_vma=False,
    )
```
